32 devices in a mesh: dp: 4 (over y, x), fsdp: 8 (over z, core).
Axes of the slice: x: 2, y: 2, z: 4, core: 2. Of those that a mesh axis runs over, the one named last changes fastest.
Arguments:
- tokens: bfloat16 [4096, 2048], P(('dp', 'fsdp')), may hold values from -6 to 6
- out_cotangent: bfloat16 [4096, 2048], P(('dp', 'fsdp')), may hold values from -6 to 6
- counts: int32 [4, 8], P('dp', 'fsdp'), may hold values from 64 to 128, as said below
- forget_gap: float32 [2048], replicated, may hold values from 4.8828126e-05 to 0.5
- mixer_weight: float32 [2048, 4, 2048], P(('dp', 'fsdp')), may hold values from -0.15909903 to 0.15909903
- expand_weight: float32 [2048, 2, 5632], P(('dp', 'fsdp')), may hold values from -0.15909903 to 0.15909903
- shrink_weight: float32 [5632, 2048], P(('dp', 'fsdp')), may hold values from -0.09594032 to 0.09594032
- norm_gains: float32 [3, 2048], replicated, may hold values from 0.5 to 1.5
- mixer_first: float32 [2048, 4, 2048], P(('dp', 'fsdp')), may hold values from -23.04 to 23.04
- mixer_second: float32 [2048, 4, 2048], P(('dp', 'fsdp')), may hold values from 0.458752 to 3.670016
- expand_first: float32 [2048, 2, 5632], P(('dp', 'fsdp')), may hold values from -23.04 to 23.04
- expand_second: float32 [2048, 2, 5632], P(('dp', 'fsdp')), may hold values from 0.458752 to 3.670016
- shrink_first: float32 [5632, 2048], P(('dp', 'fsdp')), may hold values from -23.04 to 23.04
- shrink_second: float32 [5632, 2048], P(('dp', 'fsdp')), may hold values from 0.458752 to 3.670016
- gains_first: float32 [3, 2048], replicated, may hold values from -16 to 16
- gains_second: float32 [3, 2048], replicated, may hold values from 0.65536 to 2.62144
Outputs:
- block_output: bfloat16 [4096, 2048], P(('dp', 'fsdp'))
- token_grad: bfloat16 [4096, 2048], P(('dp', 'fsdp'))
- mixer_grad: float32 [2048, 4, 2048], P(('dp', 'fsdp'))
- mixer_first_new: float32 [2048, 4, 2048], P(('dp', 'fsdp'))
- mixer_second_new: float32 [2048, 4, 2048], P(('dp', 'fsdp'))
- mixer_weight_new: float32 [2048, 4, 2048], P(('dp', 'fsdp'))
- expand_grad: float32 [2048, 2, 5632], P(('dp', 'fsdp'))
- expand_first_new: float32 [2048, 2, 5632], P(('dp', 'fsdp'))
- expand_second_new: float32 [2048, 2, 5632], P(('dp', 'fsdp'))
- expand_weight_new: float32 [2048, 2, 5632], P(('dp', 'fsdp'))
- shrink_grad: float32 [5632, 2048], P(('dp', 'fsdp'))
- shrink_first_new: float32 [5632, 2048], P(('dp', 'fsdp'))
- shrink_second_new: float32 [5632, 2048], P(('dp', 'fsdp'))
- shrink_weight_new: float32 [5632, 2048], P(('dp', 'fsdp'))
- gains_grad: float32 [3, 2048], replicated
- gains_first_new: float32 [3, 2048], replicated
- gains_second_new: float32 [3, 2048], replicated
- gains_new: float32 [3, 2048], replicated
- trust_norms: float32 [2, 10], replicated
The draws below stay inside these ranges and needn't reach their ends.
Inputs may be any that keep to these rules, and one draw needn't show every extreme that they name: `counts`: every device holds at least 64 tokens; in one group, drawn from the seed, every device is full.
All inputs are finite; a program needn't handle non-finite values.
Results may differ from the reference program's by a relative error of at most 0.011.
Values may be sent and summed in bfloat16 or wider, within the bound.
No kernel may reach another device: no remote copies, remote signals or barrier semaphores. Data moves between devices by JAX's collectives and lax.ppermute only.
A program may use at most 576 MiB of HBM per device.

```python
import math
import jax
import jax.numpy as jnp
from jax import lax

D = 2048
FF = 5632
TOK_DEV = 128
STEP = 10
GROUPS = 4
SPAN = 8
STREAM = 1024
TOKENS = 4096


def row_factor(rows, low_end, high_end):
    place = jnp.arange(rows, dtype=jnp.float32) / max(rows - 1, 1)
    return low_end * (high_end / low_end) ** place


def grad_size():
    return 0.4 * TOKENS ** 0.5


def draw_counts(key, part):
    key = jax.random.fold_in(key, 11)
    first_key, second_key = jax.random.split(key)
    drawn = jax.random.randint(first_key, (GROUPS, SPAN), TOK_DEV // 2, TOK_DEV + 1)
    full_group = jax.random.randint(second_key, (), 0, GROUPS)
    rows = jnp.arange(GROUPS, dtype=jnp.int32)[:, None]
    return jnp.where(rows == full_group, TOK_DEV, drawn).astype(jnp.int32)


def draw_mixer_weight(key, part):
    key = jax.random.fold_in(key, 21)
    shape = (D, 4, D)
    unit = jnp.clip(jax.random.normal(key, shape, jnp.float32), -4.0, 4.0)
    return unit * D ** (-0.5) * row_factor(D, 0.6, 1.8)[:, None, None]


def draw_expand_weight(key, part):
    key = jax.random.fold_in(key, 22)
    shape = (D, 2, FF)
    unit = jnp.clip(jax.random.normal(key, shape, jnp.float32), -4.0, 4.0)
    return unit * D ** (-0.5) * row_factor(D, 0.6, 1.8)[:, None, None]


def draw_shrink_weight(key, part):
    key = jax.random.fold_in(key, 23)
    shape = (FF, D)
    unit = jnp.clip(jax.random.normal(key, shape, jnp.float32), -4.0, 4.0)
    return unit * FF ** (-0.5) * row_factor(FF, 0.6, 1.8)[:, None]


def draw_mixer_first(key, part):
    key = jax.random.fold_in(key, 31)
    shape = (D, 4, D)
    unit = jnp.clip(jax.random.normal(key, shape, jnp.float32), -4.0, 4.0)
    return unit * grad_size() / 9.0 * row_factor(D, 0.5, 2.0)[:, None, None]


def draw_expand_first(key, part):
    key = jax.random.fold_in(key, 32)
    shape = (D, 2, FF)
    unit = jnp.clip(jax.random.normal(key, shape, jnp.float32), -4.0, 4.0)
    return unit * grad_size() / 9.0 * row_factor(D, 0.5, 2.0)[:, None, None]


def draw_shrink_first(key, part):
    key = jax.random.fold_in(key, 33)
    shape = (FF, D)
    unit = jnp.clip(jax.random.normal(key, shape, jnp.float32), -4.0, 4.0)
    return unit * grad_size() / 9.0 * row_factor(FF, 0.5, 2.0)[:, None]


def draw_mixer_second(key, part):
    key = jax.random.fold_in(key, 41)
    spread = jax.random.uniform(key, (D, 4, D), jnp.float32, 0.7, 1.4)
    return 0.001 * grad_size() ** 2 * spread * row_factor(D, 4.0, 1.0)[:, None, None]


def draw_expand_second(key, part):
    key = jax.random.fold_in(key, 42)
    spread = jax.random.uniform(key, (D, 2, FF), jnp.float32, 0.7, 1.4)
    return 0.001 * grad_size() ** 2 * spread * row_factor(D, 4.0, 1.0)[:, None, None]


def draw_shrink_second(key, part):
    key = jax.random.fold_in(key, 43)
    spread = jax.random.uniform(key, (FF, D), jnp.float32, 0.7, 1.4)
    return 0.001 * grad_size() ** 2 * spread * row_factor(FF, 4.0, 1.0)[:, None]


def levels(stream_key, dims, cuts, smallest, largest):
    loudness = 1.0
    for position, blocks in cuts:
        steps = jax.random.uniform(jax.random.fold_in(jax.random.fold_in(stream_key, 6), position), (blocks,), jnp.float32, smallest / len(cuts), largest / len(cuts))
        loudness = loudness * jnp.repeat(jnp.exp(steps), dims[position] // blocks).reshape((-1,) + (1,) * (len(dims) - 1 - position))
    return loudness


def centred(own_key, extent, deviation, bound, cuts=(), held_as=jnp.bfloat16):
    values = jax.random.normal(own_key, extent, jnp.float32) * deviation
    if len(cuts) > 0:
        values = levels(own_key, extent, cuts, -0.22, 0.18) * values
    return jnp.clip(values, min=-bound, max=bound).astype(held_as)


def setup_inputs(seed: int = 0) -> dict:
    keys = jax.random.split(jax.random.key(seed), 17)
    return {
        "tokens": centred(keys[0], (TOKENS, D), 1.0, 6.0, ((0, 32),)),
        "out_cotangent": centred(keys[1], (TOKENS, D), 1.0, 6.0, ((0, 32),)),
        "counts": draw_counts(jax.random.fold_in(keys[16], 71), 0),
        "forget_gap": jnp.clip(jnp.exp(jax.random.uniform(keys[3], (D,), jnp.float32, math.log(4.882812572759576e-05), math.log(0.5))), 4.882812572759576e-05, 0.5),
        "mixer_weight": draw_mixer_weight(jax.random.fold_in(keys[16], 71), 0),
        "expand_weight": draw_expand_weight(jax.random.fold_in(keys[16], 71), 0),
        "shrink_weight": draw_shrink_weight(jax.random.fold_in(keys[16], 71), 0),
        "norm_gains": jnp.clip(1.0 + 0.1 * jax.random.normal(keys[7], (3, D), jnp.float32), 0.5, 1.5),
        "mixer_first": draw_mixer_first(jax.random.fold_in(keys[16], 71), 0),
        "mixer_second": draw_mixer_second(jax.random.fold_in(keys[16], 71), 0),
        "expand_first": draw_expand_first(jax.random.fold_in(keys[16], 71), 0),
        "expand_second": draw_expand_second(jax.random.fold_in(keys[16], 71), 0),
        "shrink_first": draw_shrink_first(jax.random.fold_in(keys[16], 71), 0),
        "shrink_second": draw_shrink_second(jax.random.fold_in(keys[16], 71), 0),
        "gains_first": centred(keys[14], (3, D), (0.4 * TOKENS ** 0.5 / 9), 16.0, (), jnp.float32),
        "gains_second": jnp.clip(jnp.exp(jax.random.uniform(keys[15], (3, D), jnp.float32, math.log(0.65536), math.log(2.62144))), 0.65536, 2.62144),
    }


@jax.custom_vjp
def low(v):
    return lax.optimization_barrier(v.astype(jnp.bfloat16)).astype(jnp.float32)

@jax.custom_vjp
def low_back(v):
    return v

def low_keep(v):
    return (low(v), None)

def low_pass(kept, grad):
    return (grad,)

def back_keep(v):
    return (v, None)

def back_low(kept, grad):
    return (low(grad),)
low.defvjp(low_keep, low_pass)
low_back.defvjp(back_keep, back_low)
highest = lax.Precision.HIGHEST
norm_eps = 1e-06
beta_one = 0.9
beta_two = 0.999
adam_eps = 1e-06
decay_rate = 0.01
learn_rate = 0.3

def rms_scale(values):
    return lax.rsqrt(lax.optimization_barrier(jnp.mean(values * values, axis=-1, keepdims=True)) + norm_eps)

def link(first, second):
    return (first[0] * second[0], second[0] * first[1] + second[1])

def forward_group(tokens_f, mixer, expand, shrink, gains, valid_rows, forget_gap):
    mixer_low = low(mixer)
    expand_low = low(expand)
    shrink_low = low(shrink)
    input_low = low(tokens_f * rms_scale(tokens_f) * gains[0])
    projected = low_back(jnp.einsum('td,dke->tke', input_low, mixer_low[:, :3], precision=highest))
    in_logit = projected[:, 0]
    forget_logit = projected[:, 1]
    out_logit = projected[:, 2]
    intake = forget_gap * (1.0 - jax.nn.sigmoid(forget_logit)) * valid_rows
    forget = 1.0 - intake
    inflow = jax.nn.silu(in_logit) * intake
    hidden_seq = lax.associative_scan(link, (forget, inflow), axis=0)[1]
    mix_low = low(hidden_seq * rms_scale(hidden_seq) * gains[1] * jax.nn.silu(out_logit))
    mixed = low_back(jnp.dot(mix_low, mixer_low[:, 3], precision=highest))
    residual = tokens_f + mixed
    feed_low = low(residual * rms_scale(residual) * gains[2])
    expanded = low_back(jnp.einsum('td,dkf->tkf', feed_low, expand_low, precision=highest))
    product_low = low(jax.nn.silu(expanded[:, 0]) * expanded[:, 1])
    return (residual + jnp.dot(product_low, shrink_low, precision=highest)) * valid_rows

def lamb(weight, grad, first, second, axes):
    bias_one = 1.0 - beta_one ** STEP
    bias_two = 1.0 - beta_two ** STEP
    first_new = beta_one * first + (1.0 - beta_one) * grad
    second_new = beta_two * second + (1.0 - beta_two) * grad * grad
    update = first_new / bias_one / (jnp.sqrt(second_new / bias_two) + adam_eps) + decay_rate * weight
    weight_norm = jnp.sqrt(lax.optimization_barrier(jnp.sum(weight * weight, axis=axes, keepdims=True)))
    update_norm = jnp.sqrt(lax.optimization_barrier(jnp.sum(update * update, axis=axes, keepdims=True)))
    weight_new = weight - learn_rate * (weight_norm / (update_norm + adam_eps)) * update
    return (first_new, second_new, weight_new, weight_norm.reshape(-1), update_norm.reshape(-1))

def reference(tokens, out_cotangent, counts, forget_gap, mixer_weight, expand_weight, shrink_weight, norm_gains, mixer_first, mixer_second, expand_first, expand_second, shrink_first, shrink_second, gains_first, gains_second):
    slots = jnp.arange(TOK_DEV, dtype=jnp.int32)
    valid_all = (slots[None, None, :] < counts[:, :, None]).astype(jnp.float32).reshape(GROUPS, STREAM, 1)
    token_groups = tokens.astype(jnp.float32).reshape(GROUPS, STREAM, D)
    cotangent_groups = out_cotangent.astype(jnp.float32).reshape(GROUPS, STREAM, D)

    def per_group(totals, item):
        group_tokens, group_cotangent, valid_rows = item

        def forward(tokens_f, mixer, expand, shrink, gains):
            return forward_group(tokens_f, mixer, expand, shrink, gains, valid_rows, forget_gap)
        output, pullback = jax.vjp(forward, group_tokens, mixer_weight, expand_weight, shrink_weight, norm_gains)
        grads = pullback(group_cotangent)
        totals = tuple((total + grad for total, grad in zip(totals, grads[1:])))
        return (totals, (output.astype(jnp.bfloat16), grads[0].astype(jnp.bfloat16)))
    start = (jnp.zeros_like(mixer_weight), jnp.zeros_like(expand_weight), jnp.zeros_like(shrink_weight), jnp.zeros_like(norm_gains))
    totals, (outputs, input_grads) = lax.scan(per_group, start, (token_groups, cotangent_groups, valid_all))
    mixer_grad, expand_grad, shrink_grad, gains_grad = totals
    mixer_res = lamb(mixer_weight, mixer_grad, mixer_first, mixer_second, (0, 2))
    expand_res = lamb(expand_weight, expand_grad, expand_first, expand_second, (0, 2))
    shrink_res = lamb(shrink_weight, shrink_grad, shrink_first, shrink_second, (0, 1))
    gains_res = lamb(norm_gains, gains_grad, gains_first, gains_second, (1,))
    weight_norms = jnp.concatenate([mixer_res[3], expand_res[3], shrink_res[3], gains_res[3]])
    update_norms = jnp.concatenate([mixer_res[4], expand_res[4], shrink_res[4], gains_res[4]])
    trust_norms = jnp.stack([weight_norms, update_norms])
    return (outputs.reshape(TOKENS, D), input_grads.reshape(TOKENS, D), mixer_grad, mixer_res[0], mixer_res[1], mixer_res[2], expand_grad, expand_res[0], expand_res[1], expand_res[2], shrink_grad, shrink_res[0], shrink_res[1], shrink_res[2], gains_grad, gains_res[0], gains_res[1], gains_res[2], trust_norms)
```

```python
import functools

import jax
import jax.numpy as jnp
from jax import lax
from jax.experimental import pallas as pl
from jax.experimental.pallas import tpu as pltpu
from jax.sharding import PartitionSpec as P

STEP = 10


norm_eps = 1e-06
beta_one = 0.9
beta_two = 0.999
adam_eps = 1e-06
decay_rate = 0.01
learn_rate = 0.3

f32 = jnp.float32
bf16 = jnp.bfloat16

EXTRA = 128
TILE = 8
WIDE = 32
CHUNK = 64
VMEM_BYTES = 48 * 1024 * 1024


def rms_scale(values):
    return lax.rsqrt(jnp.mean(values * values, axis=-1, keepdims=True) + norm_eps)


def rms_back(upstream, normed, scale):
    return scale * (upstream - normed * jnp.mean(upstream * normed, axis=-1, keepdims=True))


def silu_slope(values):
    squashed = jax.nn.sigmoid(values)
    return squashed * (1.0 + values * (1.0 - squashed))


def squares_of(matrices):
    return jnp.sum(matrices * matrices, axis=(0, 2))


def adam_direction(weight, grad, first, second):
    bias_one = 1.0 - beta_one**STEP
    bias_two = 1.0 - beta_two**STEP
    first_new = beta_one * first + (1.0 - beta_one) * grad
    second_new = beta_two * second + (1.0 - beta_two) * grad * grad
    update = (
        first_new / bias_one / (jnp.sqrt(second_new / bias_two) + adam_eps) + decay_rate * weight
    )
    return (first_new, second_new, update)


def apply_trust(weight, update, weight_sq, update_sq, shape):
    ratio = jnp.sqrt(weight_sq) / (jnp.sqrt(update_sq) + adam_eps)
    return weight - learn_rate * ratio.reshape(shape) * update


def split_low(column):
    head = lax.reduce_precision(column, 8, 7)
    return jnp.concatenate([head, column - head], axis=1).astype(bf16)


def pad_columns(columns):
    return jnp.pad(columns, ((0, 0), (0, EXTRA - columns.shape[1])))


def tile_scan(decay, inflow, reverse):
    rows = decay.shape[0]
    place = lax.broadcasted_iota(jnp.int32, decay.shape, 0)
    shift = 1
    while shift < rows:
        amount = rows - shift if reverse else shift
        reached = place < rows - shift if reverse else place >= shift
        earlier_decay = jnp.where(reached, pltpu.roll(decay, amount, 0), 1.0)
        earlier_inflow = jnp.where(reached, pltpu.roll(inflow, amount, 0), 0.0)
        inflow = inflow + decay * earlier_inflow
        decay = decay * earlier_decay
        shift *= 2
    return decay, inflow


def by_chunks(rows, work):
    def step(i, nothing):
        work(pl.ds(pl.multiple_of(i * CHUNK, CHUNK), CHUNK))
        return nothing

    lax.fori_loop(0, rows // CHUNK, step, 0)


def tile_row(i, tile, core, slots, groups):
    block = lax.div(i, slots // tile)
    first = lax.rem(block + core, 2) * groups * slots
    return first + lax.rem(i, slots // tile) * tile


def tile_at(first, b, tile, slots):
    return pl.ds(pl.multiple_of(first + b * slots, tile), tile)


def recur_forward_kernel(
    core_ref, logits_ref, valid_ref, gap_ref, decay_ref, local_ref, ends_ref
):
    rows, width = local_ref.shape
    groups = ends_ref.shape[0] // 2
    slots = rows // (2 * groups)

    def gates(at):
        in_logit = logits_ref[at, pl.ds(0, width)]
        closed = 1.0 - jax.nn.sigmoid(logits_ref[at, pl.ds(width, width)])
        intake = gap_ref[...] * closed * valid_ref[at, :]
        decay_ref[at, :] = 1.0 - intake
        local_ref[at, :] = in_logit * jax.nn.sigmoid(in_logit) * intake

    by_chunks(rows, gates)

    def step(i, carried):
        first = tile_row(i, TILE, core_ref[0], slots, groups)
        after_tile = []
        for b, (carry_decay, carry) in enumerate(carried):
            at = tile_at(first, b, TILE, slots)
            decay, local = tile_scan(decay_ref[at, :], local_ref[at, :], False)
            hidden = local + decay * carry
            decay = decay * carry_decay
            decay_ref[at, :] = decay
            local_ref[at, :] = hidden
            after_tile.append((decay[TILE - 1 :, :], hidden[TILE - 1 :, :]))
        return tuple(after_tile)

    start = (jnp.ones((1, width), f32), jnp.zeros((1, width), f32))
    ends = lax.fori_loop(0, 2 * slots // TILE, step, (start,) * groups)
    ends_ref[...] = jnp.concatenate([end[0] for end in ends] + [end[1] for end in ends], axis=0)


def recur_mix_kernel(
    core_ref,
    logits_ref,
    decay_ref,
    local_ref,
    carry_ref,
    gain_ref,
    hidden_ref,
    before_ref,
    mix_ref,
    squares_ref,
):
    rows, width = local_ref.shape
    groups = carry_ref.shape[0]
    slots = rows // (2 * groups)

    def step(i, carried):
        first = tile_row(i, WIDE, core_ref[0], slots, groups)
        after_tile = []
        for b in range(groups):
            at = tile_at(first, b, WIDE, slots)
            hidden = local_ref[at, :] + decay_ref[at, :] * carry_ref[b : b + 1, :]
            place = lax.broadcasted_iota(jnp.int32, hidden.shape, 0)
            out_logit = logits_ref[at, pl.ds(2 * width, width)]
            swish = out_logit * jax.nn.sigmoid(out_logit)
            hidden_ref[at, :] = hidden
            before_ref[at, :] = jnp.where(place > 0, pltpu.roll(hidden, 1, 0), carried[b])
            squares_ref[at, :] = jnp.sum(hidden * hidden, axis=1, keepdims=True)
            mix_ref[at, :] = (hidden * gain_ref[...] * swish).astype(bf16)
            after_tile.append(hidden[WIDE - 1 :, :])
        return tuple(after_tile)

    start = tuple(carry_ref[b : b + 1, :] for b in range(groups))
    lax.fori_loop(0, 2 * slots // WIDE, step, start)


def recur_reverse_kernel(
    core_ref,
    logits_ref,
    hidden_ref,
    grad_mix_ref,
    valid_ref,
    scale_ref,
    mean_ref,
    gap_ref,
    gain_ref,
    decay_ref,
    local_ref,
    out_grad_ref,
    mix_ref,
    ends_ref,
    gain_grad_ref,
):
    rows, width = local_ref.shape
    groups = ends_ref.shape[0] // 2
    slots = rows // (2 * groups)
    gain_grad_ref[...] = jnp.zeros_like(gain_grad_ref)

    def gates(at):
        scale = scale_ref[at, :]
        out_logit = logits_ref[at, pl.ds(2 * width, width)]
        closed = 1.0 - jax.nn.sigmoid(logits_ref[at, pl.ds(width, width)])
        decay_ref[at, :] = 1.0 - gap_ref[...] * closed * valid_ref[at, :]
        squashed = jax.nn.sigmoid(out_logit)
        swish = out_logit * squashed
        slope = squashed * (1.0 + out_logit * (1.0 - squashed))
        normed = hidden_ref[at, :] * scale
        grad_mix = grad_mix_ref[at, :]
        through = grad_mix * normed
        gain_grad_ref[...] += jnp.sum(through * swish, axis=0, keepdims=True)
        out_grad_ref[at, :] = (through * gain_ref[...] * slope).astype(bf16)
        mix_ref[at, :] = (normed * gain_ref[...] * swish).astype(bf16)
        local_ref[at, :] = scale * (grad_mix * gain_ref[...] * swish - normed * mean_ref[at, :])

    by_chunks(rows, gates)
    tiles = 2 * slots // TILE

    def step(k, carried):
        first = tile_row(tiles - 1 - k, TILE, core_ref[0], slots, groups)
        after_tile = []
        for b, (carry_decay, carry, later) in enumerate(carried):
            at = tile_at(first, b, TILE, slots)
            forget = decay_ref[at, :]
            place = lax.broadcasted_iota(jnp.int32, forget.shape, 0)
            decay = jnp.where(place < TILE - 1, pltpu.roll(forget, TILE - 1, 0), later)
            decay, local = tile_scan(decay, local_ref[at, :], True)
            adjoint = local + decay * carry
            decay = decay * carry_decay
            decay_ref[at, :] = decay
            local_ref[at, :] = adjoint
            after_tile.append((decay[:1, :], adjoint[:1, :], forget[:1, :]))
        return tuple(after_tile)

    one = jnp.ones((1, width), f32)
    ends = lax.fori_loop(0, tiles, step, ((one, jnp.zeros((1, width), f32), one),) * groups)
    ends_ref[...] = jnp.concatenate(
        [end[0] * end[2] for end in ends] + [end[1] * end[2] for end in ends], axis=0
    )


def recur_finish_kernel(
    logits_ref,
    before_ref,
    valid_ref,
    decay_ref,
    local_ref,
    carry_ref,
    out_grad_ref,
    gap_ref,
    grad_ref,
):
    rows, width = local_ref.shape
    groups = carry_ref.shape[0]
    slots = rows // (2 * groups)

    def step(i, nothing):
        for block in range(2 * groups):
            at = pl.ds(pl.multiple_of(block * slots + i * WIDE, WIDE), WIDE)
            carry = carry_ref[block % groups : block % groups + 1, :]
            adjoint = local_ref[at, :] + decay_ref[at, :] * carry
            in_logit = logits_ref[at, pl.ds(0, width)]
            squashed = jax.nn.sigmoid(logits_ref[at, pl.ds(width, width)])
            in_squashed = jax.nn.sigmoid(in_logit)
            in_slope = in_squashed * (1.0 + in_logit * (1.0 - in_squashed))
            weighted = gap_ref[...] * valid_ref[at, :] * (1.0 - squashed) * adjoint
            into = (weighted * in_slope).astype(bf16)
            forget = weighted * squashed * (before_ref[at, :] - in_logit * in_squashed)
            grad_ref[at, :] = jnp.concatenate(
                [into, forget.astype(bf16), out_grad_ref[at, :]], axis=1
            )
        return nothing

    lax.fori_loop(0, slots // WIDE, step, 0)


def finish_input_kernel(groups, chips, tokens_ref, gains_ref, residual_ref, *refs):
    part_refs, grad_ref, gain_grad_ref = refs[:-2], refs[-2], refs[-1]
    total = part_refs[0][...].astype(f32)
    for part_ref in part_refs[1:]:
        total = total + part_ref[...].astype(f32)
    piece = total.shape[1] // (groups * chips)
    grad = jnp.concatenate(
        [
            total[:, (z * groups + g) * piece : (z * groups + g + 1) * piece]
            for g in range(groups)
            for z in range(chips)
        ],
        axis=1,
    )
    inputs = tokens_ref[...].astype(f32)
    scale = rms_scale(inputs)
    normed = inputs * scale
    gain_grad_ref[...] = jnp.sum(grad * normed, axis=0, keepdims=True)
    grad_ref[...] = (
        residual_ref[...] + rms_back(grad * gains_ref[0:1, :], normed, scale)
    ).astype(bf16)


def call_kernel(kernel, name, shapes, scalar, *args):
    specs = [pl.BlockSpec(memory_space=pltpu.VMEM)] * len(args)
    if scalar is not None:
        specs, args = [pl.BlockSpec(memory_space=pltpu.SMEM)] + specs, (scalar,) + args
    return pl.pallas_call(
        kernel,
        out_shape=[jax.ShapeDtypeStruct(shape, kind) for shape, kind in shapes],
        in_specs=specs,
        compiler_params=pltpu.CompilerParams(vmem_limit_bytes=VMEM_BYTES),
        name=name,
    )(*args)


SEQUENCE = ("z", "core")
PLANE = ("dp", "core")


def gather_tokens(part):
    return lax.all_gather(part, SEQUENCE, axis=0, tiled=True)


def scatter_tokens(whole):
    return lax.psum_scatter(whole, SEQUENCE, scatter_dimension=0, tiled=True).astype(f32)


def gather_chips(part):
    return lax.all_gather(part, "z", axis=0, tiled=True)


def scatter_chips(whole):
    return lax.psum_scatter(whole, "z", scatter_dimension=0, tiled=True)


def swap(blocks, axes):
    return lax.all_to_all(blocks, axes, split_axis=0, concat_axis=0, tiled=True)


def gather_plane(part, *earlier):
    near = jnp.concatenate(gather_groups(part), axis=0)
    if earlier:
        near = after(near, *earlier)
    return jnp.concatenate([near, flip(near, "core", 1)], axis=0), near


def scatter_plane(whole, *earlier):
    half, groups = whole.shape[0] // 2, lax.axis_size("dp")
    near = add_low(whole[:half], flip(whole[half:], "core", 1))
    slots = half // groups
    return scatter_groups(
        [near[b * slots : (b + 1) * slots] for b in range(groups)], *earlier
    )


def chain_chips(ends, reverse):
    chips, here = lax.axis_size("z"), lax.axis_index("z")
    count = ends.shape[0] // 2
    carry = jnp.zeros_like(ends[:count])
    for far in range(chips - 1, 0, -1):
        step = -far if reverse else far
        there = lax.ppermute(ends, "z", [(i, (i + step) % chips) for i in range(chips)])
        reached = here + far < chips if reverse else here >= far
        carry = jnp.where(reached, there[count:] + there[:count] * carry, carry)
    return carry


def flip(part, axis, bit):
    count = lax.axis_size(axis)
    return lax.ppermute(part, axis, [(i, i ^ bit) for i in range(count)])


def bits_of(axis):
    return [1 << k for k in range(lax.axis_size(axis).bit_length() - 1)]


def half_rows(rows):
    return -(-rows // 32) * 16


def gather_groups(part, *earlier):
    if lax.axis_size("dp") == 4:
        half = half_rows(part.shape[0])
        one, two = flip(part, "dp", 1), flip(part, "dp", 2)
        if earlier:
            one, two = after(one, *earlier), after(two, *earlier)
        three = jnp.concatenate(
            [flip(one[:half], "dp", 2), flip(two[half:], "dp", 1)], axis=0
        )
        return [part, one, two, three]
    blocks = [part]
    for bit in bits_of("dp"):
        blocks = blocks + [flip(block, "dp", bit) for block in blocks]
    return blocks


def scatter_groups(blocks, *earlier):
    if len(blocks) == 4:
        half = half_rows(blocks[0].shape[0])
        upper = flip(blocks[3][:half], "dp", 1)
        lower = flip(blocks[3][half:], "dp", 2)
        two = jnp.concatenate([add_low(blocks[2][:half], upper), blocks[2][half:]], axis=0)
        one = jnp.concatenate([blocks[1][:half], add_low(blocks[1][half:], lower)], axis=0)
        if earlier:
            one, two = after(one, *earlier), after(two, *earlier)
        return [blocks[0], flip(one, "dp", 1), flip(two, "dp", 2)]
    for bit in reversed(bits_of("dp")):
        blocks = [
            add_low(block, flip(other, "dp", bit))
            for block, other in zip(blocks[:bit], blocks[bit:])
        ]
    return blocks


def add_parts(parts):
    total = parts[0].astype(f32)
    for part in parts[1:]:
        total = total + part.astype(f32)
    return total


def add_low(left, right):
    return (left.astype(f32) + right.astype(f32)).astype(bf16)


def sum_over(part, axes):
    for axis in axes:
        for bit in bits_of(axis):
            part = part + flip(part, axis, bit)
    return part


def place_groups(blocks):
    group, rows = lax.axis_index("dp"), blocks[0].shape[0]
    whole = jnp.zeros((len(blocks) * rows,) + blocks[0].shape[1:], blocks[0].dtype)
    for b, block in enumerate(blocks):
        whole = lax.dynamic_update_slice_in_dim(whole, block, (group ^ b) * rows, 0)
    return whole


def take_groups(whole, axis):
    count, group = lax.axis_size("dp"), lax.axis_index("dp")
    size = whole.shape[axis] // count
    return [
        lax.dynamic_slice_in_dim(whole, (group ^ b) * size, size, axis) for b in range(count)
    ]


def sequence_pieces():
    groups, peers = lax.axis_size("dp"), lax.axis_size("z") * 2
    return [[g * peers + j for g in range(groups)] for j in range(peers)]


def plane_pieces():
    groups, chips = lax.axis_size("dp"), lax.axis_size("z")
    return [
        [(g * chips + z) * 2 + core for z in range(chips)]
        for g in range(groups)
        for core in range(2)
    ]


def split_kernel(kinds, piece, table, weight_ref, split_ref, *rest_refs):
    rows, every, depth = weight_ref.shape
    whole = [weight_ref[:, k, :] for k in range(every)]
    for j, pieces in enumerate(table):
        own = [
            whole[k][:, p * piece : (p + 1) * piece] for k in range(kinds) for p in pieces
        ]
        split_ref[j * rows : (j + 1) * rows, :] = jnp.concatenate(own, axis=1).astype(bf16)
    for k, rest_ref in zip(range(kinds, every), rest_refs):
        part = depth // len(table)
        for j in range(len(table)):
            rest_ref[j * rows : (j + 1) * rows, :] = whole[k][
                :, j * part : (j + 1) * part
            ].astype(bf16)


def split_columns(weight, kinds, piece, table):
    rows, every, depth = weight.shape
    shapes = [jax.ShapeDtypeStruct((len(table) * rows, kinds * len(table[0]) * piece), bf16)]
    shapes += [
        jax.ShapeDtypeStruct((len(table) * rows, depth // len(table)), bf16)
    ] * (every - kinds)
    return pl.pallas_call(
        functools.partial(split_kernel, kinds, piece, table),
        out_shape=shapes,
        compiler_params=pltpu.CompilerParams(vmem_limit_bytes=VMEM_BYTES),
        name="split_columns",
    )(weight)


def join_kernel(kinds, piece, table, own_ref, *refs):
    rest_refs, out_ref = refs[:-1], refs[-1]
    rows, every, depth = out_ref.shape
    place = {p: (j, q) for j, pieces in enumerate(table) for q, p in enumerate(pieces)}
    count = len(table[0])
    own = [own_ref[j * rows : (j + 1) * rows, :].astype(f32) for j in range(len(table))]
    for k in range(kinds):
        pieces = []
        for p in range(len(place)):
            j, q = place[p]
            pieces.append(own[j][:, (k * count + q) * piece : (k * count + q + 1) * piece])
        out_ref[:, k, :] = jnp.concatenate(pieces, axis=1)
    for k, rest_ref in zip(range(kinds, every), rest_refs):
        out_ref[:, k, :] = rest_ref[...]


def join_columns(own, kinds, piece, table, *rest):
    shape = (own.shape[0] // len(table), kinds + len(rest), len(table) * len(table[0]) * piece)
    return pl.pallas_call(
        functools.partial(join_kernel, kinds, piece, table),
        out_shape=jax.ShapeDtypeStruct(shape, f32),
        compiler_params=pltpu.CompilerParams(vmem_limit_bytes=VMEM_BYTES),
        name="join_columns",
    )(own, *rest)


def after_kernel(*refs):
    pass


def after(value, *earlier):
    return pl.pallas_call(
        after_kernel,
        out_shape=jax.ShapeDtypeStruct(value.shape, value.dtype),
        in_specs=[pl.BlockSpec(memory_space=pl.ANY)] * (1 + len(earlier)),
        out_specs=pl.BlockSpec(memory_space=pl.ANY),
        input_output_aliases={0: 0},
        name="after",
    )(value, *earlier)


def dot(left, right, dims):
    return lax.dot_general(left, right, (dims, ((), ())), preferred_element_type=f32)


def body(
    tokens,
    out_cotangent,
    counts,
    forget_gap,
    mixer_weight,
    expand_weight,
    shrink_weight,
    norm_gains,
    mixer_first,
    mixer_second,
    expand_first,
    expand_second,
    shrink_first,
    shrink_second,
    gains_first,
    gains_second,
):
    nd, chips = lax.axis_size("dp"), lax.axis_size("z")
    group, core = lax.axis_index("dp"), lax.axis_index("core")
    slots, depth = tokens.shape
    rows = mixer_weight.shape[0]
    hid_rows = shrink_weight.shape[0]
    width = chips * rows
    hid = nd * hid_rows
    plane_rows = 2 * nd * slots
    core_low = core.astype(jnp.int32).reshape(1)

    def own_columns(vector):
        pieces = vector.reshape(nd, chips, 2, rows)
        return lax.dynamic_slice(pieces, (group, 0, core, 0), (1, chips, 1, rows)).reshape(1, width)

    def turn(whole, first, second):
        pieces = whole.reshape(slots, first, second, 2 * rows)
        return pieces.transpose(0, 2, 1, 3).reshape(slots, depth)

    lead_blocks, trail_low = split_columns(mixer_weight, 3, rows, plane_pieces())
    (expand_blocks,) = split_columns(expand_weight, 2, hid_rows, sequence_pieces())

    valid_here = (lax.iota(jnp.int32, slots) < counts[0, 0]).astype(f32)[:, None]
    inputs = tokens.astype(f32)
    scale_one = rms_scale(inputs)
    normed_one = inputs * scale_one
    input_low = turn((normed_one * norm_gains[0]).astype(bf16), nd, chips)
    cotangent_low = (out_cotangent.astype(f32) * valid_here).astype(bf16)

    lead_own = swap(lead_blocks, PLANE)
    input_low = jnp.concatenate([input_low, pad_columns(valid_here.astype(bf16))], axis=1)
    input_all, _ = gather_plane(after(input_low, lead_own))
    valid = input_all[:, depth : depth + 1].astype(f32)
    input_all = input_all[:, :depth]
    shrink = place_groups(gather_groups(after(shrink_weight.astype(bf16), valid)))
    mixer_own = jnp.concatenate([lead_own, trail_low], axis=1)
    cotangent_all = gather_tokens(cotangent_low)
    mixer_near = gather_chips(after(mixer_own, cotangent_all))
    mixer_near = after(mixer_near, expand_blocks, valid, shrink)
    lead = mixer_near[:, : 3 * width]
    trail = mixer_near[:, 3 * width :].reshape(chips, 2 * nd, rows, width)
    trail = trail.transpose(0, 2, 1, 3).reshape(width, depth)

    gap = own_columns(forget_gap)
    gain = own_columns(norm_gains[1])
    logits = dot(input_all, lead, ((1,), (0,)))
    square, low_square = ((plane_rows, width), f32), ((plane_rows, width), bf16)
    ends_shape = ((2 * nd, width), f32)
    decay, local, ends = call_kernel(
        recur_forward_kernel,
        "recur_forward",
        [square, square, ends_shape],
        core_low,
        logits,
        valid,
        gap,
    )
    carry = chain_chips(ends, False)
    expand_own = swap(after(expand_blocks, carry), SEQUENCE)
    hidden, before, mix, squares = call_kernel(
        recur_mix_kernel,
        "recur_mix",
        [square, square, low_square, ((plane_rows, 1), f32)],
        core_low,
        logits,
        decay,
        local,
        carry,
        gain,
    )
    mixed_part = dot(mix, trail, ((1,), (0,))).astype(bf16)
    mixed_part = jnp.concatenate([mixed_part, pad_columns(split_low(squares))], axis=1)
    mixed_sum = add_parts(scatter_plane(mixed_part, expand_own))
    expand = place_groups(gather_groups(expand_own))
    scale_two = lax.rsqrt(
        (mixed_sum[:, depth : depth + 1] + mixed_sum[:, depth + 1 : depth + 2]) / depth + norm_eps
    )
    mixed = mixed_sum[:, :depth] * scale_two
    residual = inputs + mixed
    scale_three = rms_scale(residual)
    normed_three = residual * scale_three
    feed_low = (normed_three * norm_gains[2]).astype(bf16)
    feed_all = gather_tokens(feed_low)
    expanded = dot(feed_all, expand, ((1,), (0,)))
    gate, up = expanded[:, :hid], expanded[:, hid:]
    gate_silu = jax.nn.silu(gate)
    product_low = (gate_silu * up).astype(bf16)
    grad_product = dot(cotangent_all, shrink, ((1,), (1,)))
    grad_expanded = jnp.concatenate(
        [grad_product * up * silu_slope(gate), grad_product * gate_silu], axis=1
    ).astype(bf16)
    feed_part = dot(grad_expanded, expand, ((1,), (1,))).astype(bf16)
    grad_feed = scatter_tokens(feed_part)
    gain_three = jnp.sum(grad_feed * normed_three, 0)
    grad_residual = cotangent_low.astype(f32) + rms_back(
        grad_feed * norm_gains[2], normed_three, scale_three
    )
    residual_low = grad_residual.astype(bf16)
    mean_two = jnp.mean(residual_low.astype(f32) * mixed, axis=-1, keepdims=True)
    extras = pad_columns(jnp.concatenate([split_low(scale_two), split_low(mean_two)], axis=1))

    def owner_parts(left, right):
        return [
            dot(block, right, ((0,), (0,))).astype(bf16) for block in take_groups(left, 1)
        ]

    expand_sum = add_parts(scatter_groups(owner_parts(feed_all, grad_expanded))).astype(bf16)
    expand_columns = swap(expand_sum, SEQUENCE)
    back_all, back_near = gather_plane(
        after(jnp.concatenate([residual_low, extras], axis=1), expand_sum), expand_columns
    )
    out_part = dot(product_low, shrink, ((1,), (0,))).astype(bf16)
    out_sum = scatter_tokens(after(out_part, back_near))
    block_output = ((residual + out_sum) * valid_here).astype(bf16)
    residual_back = back_all[:, :depth]
    extras = back_all[:, depth : depth + 4].astype(f32)
    scale_all = extras[:, 0:1] + extras[:, 1:2]
    mean_all = extras[:, 2:3] + extras[:, 3:4]

    grad_mix = dot(residual_back, trail, ((1,), (1,)))
    decay, local, out_grad, mix_low, ends, gain_two = call_kernel(
        recur_reverse_kernel,
        "recur_reverse",
        [square, square, low_square, low_square, ends_shape, ((1, width), f32)],
        core_low,
        logits,
        hidden,
        grad_mix,
        valid,
        scale_all,
        mean_all,
        gap,
        gain,
    )
    carry = chain_chips(ends, True)
    (grad_projected,) = call_kernel(
        recur_finish_kernel,
        "recur_finish",
        [((plane_rows, 3 * width), bf16)],
        None,
        logits,
        before,
        valid,
        decay,
        local,
        carry,
        out_grad,
        gap,
    )
    trail_part = dot(mix_low, residual_back, ((0,), (0,))).astype(bf16)
    lead_part = dot(input_all, grad_projected, ((0,), (0,))).astype(bf16)
    lead_part = after(lead_part, out_sum)
    lead_sum = scatter_chips(lead_part)
    trail_grad = scatter_chips(after(trail_part, lead_sum))
    input_part = dot(after(grad_projected, lead_part), lead, ((1,), (1,))).astype(bf16)
    input_parts = scatter_plane(input_part)
    token_grad, gain_one = call_kernel(
        functools.partial(finish_input_kernel, nd, chips),
        "finish_input",
        [((slots, depth), bf16), ((1, depth), f32)],
        None,
        tokens,
        norm_gains,
        grad_residual,
        *input_parts,
    )
    gain_one = gain_one[0]
    shrink_part = dot(product_low, after(cotangent_all, input_part), ((0,), (0,))).astype(bf16)
    shrink_grad = add_parts(scatter_groups(take_groups(shrink_part, 0)))

    expand_grad = join_columns(
        after(expand_columns, input_part), 2, hid_rows, sequence_pieces()
    )
    lead_columns = swap(lead_sum, PLANE)

    gain_two_full = lax.dynamic_update_slice(
        jnp.zeros((nd, chips, 2, rows), f32),
        gain_two.reshape(1, chips, 1, rows),
        (group, 0, core, 0),
    ).reshape(depth)
    mixer_grad = join_columns(lead_columns, 3, rows, plane_pieces(), trail_grad.astype(f32))
    expand_first_new, expand_second_new, expand_update = adam_direction(
        expand_weight, expand_grad, expand_first, expand_second
    )
    shrink_first_new, shrink_second_new, shrink_update = adam_direction(
        shrink_weight, shrink_grad, shrink_first, shrink_second
    )
    mixer_first_new, mixer_second_new, mixer_update = adam_direction(
        mixer_weight, mixer_grad, mixer_first, mixer_second
    )
    squares_here = jnp.concatenate(
        [
            squares_of(mixer_weight),
            squares_of(expand_weight),
            squares_of(shrink_weight[:, None]),
            squares_of(mixer_update),
            squares_of(expand_update),
            squares_of(shrink_update[:, None]),
        ]
    )
    summed = sum_over(
        after(
            jnp.stack([gain_one, gain_two_full, gain_three, jnp.pad(squares_here, (0, depth - 14))]),
            block_output,
        ),
        ("dp", "z", "core"),
    )
    gains_grad = summed[:3]
    weight_sq, update_sq = summed[3, :7], summed[3, 7:14]
    gains_first_new, gains_second_new, gains_update = adam_direction(
        norm_gains, gains_grad, gains_first, gains_second
    )
    mixer_weight_new = apply_trust(
        mixer_weight, mixer_update, weight_sq[0:4], update_sq[0:4], (1, 4, 1)
    )
    expand_weight_new = apply_trust(
        expand_weight, expand_update, weight_sq[4:6], update_sq[4:6], (1, 2, 1)
    )
    shrink_weight_new = apply_trust(
        shrink_weight, shrink_update, weight_sq[6], update_sq[6], (1, 1)
    )
    gain_weight_sq = jnp.sum(norm_gains * norm_gains, axis=1)
    gain_update_sq = jnp.sum(gains_update * gains_update, axis=1)
    gains_new = apply_trust(norm_gains, gains_update, gain_weight_sq, gain_update_sq, (3, 1))
    weight_norms = jnp.sqrt(jnp.concatenate([weight_sq, gain_weight_sq]))
    update_norms = jnp.sqrt(jnp.concatenate([update_sq, gain_update_sq]))
    trust_norms = jnp.stack([weight_norms, update_norms])
    return (
        block_output,
        token_grad,
        mixer_grad,
        mixer_first_new,
        mixer_second_new,
        mixer_weight_new,
        expand_grad,
        expand_first_new,
        expand_second_new,
        expand_weight_new,
        shrink_grad,
        shrink_first_new,
        shrink_second_new,
        shrink_weight_new,
        gains_grad,
        gains_first_new,
        gains_second_new,
        gains_new,
        trust_norms,
    )


def solution(mesh):
    groups, peers = mesh.devices.shape
    devices = mesh.devices.reshape(groups, peers // 2, 2)
    return jax.shard_map(
        body,
        mesh=jax.sharding.Mesh(devices, ("dp", "z", "core")),
        in_specs=(
            P(("dp", "z", "core"), None),
            P(("dp", "z", "core"), None),
            P("dp", ("z", "core")),
            P(),
            P(("dp", "z", "core"), None, None),
            P(("dp", "z", "core"), None, None),
            P(("dp", "z", "core"), None),
            P(),
            P(("dp", "z", "core"), None, None),
            P(("dp", "z", "core"), None, None),
            P(("dp", "z", "core"), None, None),
            P(("dp", "z", "core"), None, None),
            P(("dp", "z", "core"), None),
            P(("dp", "z", "core"), None),
            P(),
            P(),
        ),
        out_specs=(
            P(("dp", "z", "core"), None),
            P(("dp", "z", "core"), None),
            P(("dp", "z", "core"), None, None),
            P(("dp", "z", "core"), None, None),
            P(("dp", "z", "core"), None, None),
            P(("dp", "z", "core"), None, None),
            P(("dp", "z", "core"), None, None),
            P(("dp", "z", "core"), None, None),
            P(("dp", "z", "core"), None, None),
            P(("dp", "z", "core"), None, None),
            P(("dp", "z", "core"), None),
            P(("dp", "z", "core"), None),
            P(("dp", "z", "core"), None),
            P(("dp", "z", "core"), None),
            P(),
            P(),
            P(),
            P(),
            P(),
        ),
        check_vma=False,
    )
```

```python
import functools

import jax
import jax.numpy as jnp
from jax import lax
from jax.experimental import pallas as pl
from jax.experimental.pallas import tpu as pltpu
from jax.sharding import PartitionSpec as P

STEP = 10


norm_eps = 1e-06
beta_one = 0.9
beta_two = 0.999
adam_eps = 1e-06
decay_rate = 0.01
learn_rate = 0.3

f32 = jnp.float32
bf16 = jnp.bfloat16

EXTRA = 128
TILE = 8
WIDE = 32
CHUNK = 64
VMEM_BYTES = 48 * 1024 * 1024


def rms_scale(values):
    return lax.rsqrt(jnp.mean(values * values, axis=-1, keepdims=True) + norm_eps)


def rms_back(upstream, normed, scale):
    return scale * (upstream - normed * jnp.mean(upstream * normed, axis=-1, keepdims=True))


def silu_slope(values):
    squashed = jax.nn.sigmoid(values)
    return squashed * (1.0 + values * (1.0 - squashed))


def squares_of(matrices):
    return jnp.sum(matrices * matrices, axis=(0, 2))


def adam_direction(weight, grad, first, second):
    bias_one = 1.0 - beta_one**STEP
    bias_two = 1.0 - beta_two**STEP
    first_new = beta_one * first + (1.0 - beta_one) * grad
    second_new = beta_two * second + (1.0 - beta_two) * grad * grad
    update = (
        first_new / bias_one / (jnp.sqrt(second_new / bias_two) + adam_eps) + decay_rate * weight
    )
    return (first_new, second_new, update)


def apply_trust(weight, update, weight_sq, update_sq, shape):
    ratio = jnp.sqrt(weight_sq) / (jnp.sqrt(update_sq) + adam_eps)
    return weight - learn_rate * ratio.reshape(shape) * update


def split_low(column):
    head = lax.reduce_precision(column, 8, 7)
    return jnp.concatenate([head, column - head], axis=1).astype(bf16)


def pad_columns(columns):
    return jnp.pad(columns, ((0, 0), (0, EXTRA - columns.shape[1])))


def tile_scan(decay, inflow, reverse):
    rows = decay.shape[0]
    place = lax.broadcasted_iota(jnp.int32, decay.shape, 0)
    shift = 1
    while shift < rows:
        amount = rows - shift if reverse else shift
        reached = place < rows - shift if reverse else place >= shift
        earlier_decay = jnp.where(reached, pltpu.roll(decay, amount, 0), 1.0)
        earlier_inflow = jnp.where(reached, pltpu.roll(inflow, amount, 0), 0.0)
        inflow = inflow + decay * earlier_inflow
        decay = decay * earlier_decay
        shift *= 2
    return decay, inflow


def by_chunks(rows, work):
    def step(i, nothing):
        work(pl.ds(pl.multiple_of(i * CHUNK, CHUNK), CHUNK))
        return nothing

    lax.fori_loop(0, rows // CHUNK, step, 0)


def tile_row(i, tile, core, slots, groups):
    block = lax.div(i, slots // tile)
    first = lax.rem(block + core, 2) * groups * slots
    return first + lax.rem(i, slots // tile) * tile


def tile_at(first, b, tile, slots):
    return pl.ds(pl.multiple_of(first + b * slots, tile), tile)


def recur_forward_kernel(
    core_ref, logits_ref, valid_ref, gap_ref, decay_ref, local_ref, ends_ref
):
    rows, width = local_ref.shape
    groups = ends_ref.shape[0] // 2
    slots = rows // (2 * groups)

    def gates(at):
        in_logit = logits_ref[at, pl.ds(0, width)]
        closed = 1.0 - jax.nn.sigmoid(logits_ref[at, pl.ds(width, width)])
        intake = gap_ref[...] * closed * valid_ref[at, :]
        decay_ref[at, :] = 1.0 - intake
        local_ref[at, :] = in_logit * jax.nn.sigmoid(in_logit) * intake

    by_chunks(rows, gates)

    def step(i, carried):
        first = tile_row(i, TILE, core_ref[0], slots, groups)
        after_tile = []
        for b, (carry_decay, carry) in enumerate(carried):
            at = tile_at(first, b, TILE, slots)
            decay, local = tile_scan(decay_ref[at, :], local_ref[at, :], False)
            hidden = local + decay * carry
            decay = decay * carry_decay
            decay_ref[at, :] = decay
            local_ref[at, :] = hidden
            after_tile.append((decay[TILE - 1 :, :], hidden[TILE - 1 :, :]))
        return tuple(after_tile)

    start = (jnp.ones((1, width), f32), jnp.zeros((1, width), f32))
    ends = lax.fori_loop(0, 2 * slots // TILE, step, (start,) * groups)
    ends_ref[...] = jnp.concatenate([end[0] for end in ends] + [end[1] for end in ends], axis=0)


def recur_mix_kernel(
    core_ref,
    logits_ref,
    decay_ref,
    local_ref,
    carry_ref,
    gain_ref,
    hidden_ref,
    before_ref,
    mix_ref,
    squares_ref,
):
    rows, width = local_ref.shape
    groups = carry_ref.shape[0]
    slots = rows // (2 * groups)

    def step(i, carried):
        first = tile_row(i, WIDE, core_ref[0], slots, groups)
        after_tile = []
        for b in range(groups):
            at = tile_at(first, b, WIDE, slots)
            hidden = local_ref[at, :] + decay_ref[at, :] * carry_ref[b : b + 1, :]
            place = lax.broadcasted_iota(jnp.int32, hidden.shape, 0)
            out_logit = logits_ref[at, pl.ds(2 * width, width)]
            swish = out_logit * jax.nn.sigmoid(out_logit)
            hidden_ref[at, :] = hidden
            before_ref[at, :] = jnp.where(place > 0, pltpu.roll(hidden, 1, 0), carried[b])
            squares_ref[at, :] = jnp.sum(hidden * hidden, axis=1, keepdims=True)
            mix_ref[at, :] = (hidden * gain_ref[...] * swish).astype(bf16)
            after_tile.append(hidden[WIDE - 1 :, :])
        return tuple(after_tile)

    start = tuple(carry_ref[b : b + 1, :] for b in range(groups))
    lax.fori_loop(0, 2 * slots // WIDE, step, start)


def recur_reverse_kernel(
    core_ref,
    logits_ref,
    hidden_ref,
    grad_mix_ref,
    valid_ref,
    scale_ref,
    mean_ref,
    gap_ref,
    gain_ref,
    decay_ref,
    local_ref,
    out_grad_ref,
    mix_ref,
    ends_ref,
    gain_grad_ref,
):
    rows, width = local_ref.shape
    groups = ends_ref.shape[0] // 2
    slots = rows // (2 * groups)
    gain_grad_ref[...] = jnp.zeros_like(gain_grad_ref)

    def gates(at):
        scale = scale_ref[at, :]
        out_logit = logits_ref[at, pl.ds(2 * width, width)]
        closed = 1.0 - jax.nn.sigmoid(logits_ref[at, pl.ds(width, width)])
        decay_ref[at, :] = 1.0 - gap_ref[...] * closed * valid_ref[at, :]
        squashed = jax.nn.sigmoid(out_logit)
        swish = out_logit * squashed
        slope = squashed * (1.0 + out_logit * (1.0 - squashed))
        normed = hidden_ref[at, :] * scale
        grad_mix = grad_mix_ref[at, :]
        through = grad_mix * normed
        gain_grad_ref[...] += jnp.sum(through * swish, axis=0, keepdims=True)
        out_grad_ref[at, :] = (through * gain_ref[...] * slope).astype(bf16)
        mix_ref[at, :] = (normed * gain_ref[...] * swish).astype(bf16)
        local_ref[at, :] = scale * (grad_mix * gain_ref[...] * swish - normed * mean_ref[at, :])

    by_chunks(rows, gates)
    tiles = 2 * slots // TILE

    def step(k, carried):
        first = tile_row(tiles - 1 - k, TILE, core_ref[0], slots, groups)
        after_tile = []
        for b, (carry_decay, carry, later) in enumerate(carried):
            at = tile_at(first, b, TILE, slots)
            forget = decay_ref[at, :]
            place = lax.broadcasted_iota(jnp.int32, forget.shape, 0)
            decay = jnp.where(place < TILE - 1, pltpu.roll(forget, TILE - 1, 0), later)
            decay, local = tile_scan(decay, local_ref[at, :], True)
            adjoint = local + decay * carry
            decay = decay * carry_decay
            decay_ref[at, :] = decay
            local_ref[at, :] = adjoint
            after_tile.append((decay[:1, :], adjoint[:1, :], forget[:1, :]))
        return tuple(after_tile)

    one = jnp.ones((1, width), f32)
    ends = lax.fori_loop(0, tiles, step, ((one, jnp.zeros((1, width), f32), one),) * groups)
    ends_ref[...] = jnp.concatenate(
        [end[0] * end[2] for end in ends] + [end[1] * end[2] for end in ends], axis=0
    )


def recur_finish_kernel(
    logits_ref,
    before_ref,
    valid_ref,
    decay_ref,
    local_ref,
    carry_ref,
    out_grad_ref,
    gap_ref,
    grad_ref,
):
    rows, width = local_ref.shape
    groups = carry_ref.shape[0]
    slots = rows // (2 * groups)

    def step(i, nothing):
        for block in range(2 * groups):
            at = pl.ds(pl.multiple_of(block * slots + i * WIDE, WIDE), WIDE)
            carry = carry_ref[block % groups : block % groups + 1, :]
            adjoint = local_ref[at, :] + decay_ref[at, :] * carry
            in_logit = logits_ref[at, pl.ds(0, width)]
            squashed = jax.nn.sigmoid(logits_ref[at, pl.ds(width, width)])
            in_squashed = jax.nn.sigmoid(in_logit)
            in_slope = in_squashed * (1.0 + in_logit * (1.0 - in_squashed))
            weighted = gap_ref[...] * valid_ref[at, :] * (1.0 - squashed) * adjoint
            into = (weighted * in_slope).astype(bf16)
            forget = weighted * squashed * (before_ref[at, :] - in_logit * in_squashed)
            grad_ref[at, :] = jnp.concatenate(
                [into, forget.astype(bf16), out_grad_ref[at, :]], axis=1
            )
        return nothing

    lax.fori_loop(0, slots // WIDE, step, 0)


def finish_input_kernel(groups, chips, tokens_ref, gains_ref, residual_ref, *refs):
    part_refs, grad_ref, gain_grad_ref = refs[:-2], refs[-2], refs[-1]
    total = part_refs[0][...].astype(f32)
    for part_ref in part_refs[1:]:
        total = total + part_ref[...].astype(f32)
    piece = total.shape[1] // (groups * chips)
    grad = jnp.concatenate(
        [
            total[:, (z * groups + g) * piece : (z * groups + g + 1) * piece]
            for g in range(groups)
            for z in range(chips)
        ],
        axis=1,
    )
    inputs = tokens_ref[...].astype(f32)
    scale = rms_scale(inputs)
    normed = inputs * scale
    gain_grad_ref[...] = jnp.sum(grad * normed, axis=0, keepdims=True)
    grad_ref[...] = (
        residual_ref[...] + rms_back(grad * gains_ref[0:1, :], normed, scale)
    ).astype(bf16)


def call_kernel(kernel, name, shapes, scalar, *args):
    specs = [pl.BlockSpec(memory_space=pltpu.VMEM)] * len(args)
    if scalar is not None:
        specs, args = [pl.BlockSpec(memory_space=pltpu.SMEM)] + specs, (scalar,) + args
    return pl.pallas_call(
        kernel,
        out_shape=[jax.ShapeDtypeStruct(shape, kind) for shape, kind in shapes],
        in_specs=specs,
        compiler_params=pltpu.CompilerParams(vmem_limit_bytes=VMEM_BYTES),
        name=name,
    )(*args)


SEQUENCE = ("z", "core")
PLANE = ("dp", "core")


def gather_tokens(part):
    return lax.all_gather(part, SEQUENCE, axis=0, tiled=True)


def scatter_tokens(whole):
    return lax.psum_scatter(whole, SEQUENCE, scatter_dimension=0, tiled=True).astype(f32)


def gather_chips(part):
    return lax.all_gather(part, "z", axis=0, tiled=True)


def scatter_chips(whole):
    return lax.psum_scatter(whole, "z", scatter_dimension=0, tiled=True)


def swap(blocks, axes):
    return lax.all_to_all(blocks, axes, split_axis=0, concat_axis=0, tiled=True)


def gather_plane(part, *earlier):
    near = jnp.concatenate(gather_groups(part), axis=0)
    if earlier:
        near = after(near, *earlier)
    return jnp.concatenate([near, flip(near, "core", 1)], axis=0), near


def scatter_plane(whole, *earlier):
    half, groups = whole.shape[0] // 2, lax.axis_size("dp")
    near = add_low(whole[:half], flip(whole[half:], "core", 1))
    slots = half // groups
    return scatter_groups(
        [near[b * slots : (b + 1) * slots] for b in range(groups)], *earlier
    )


def chain_chips(ends, reverse):
    chips, here = lax.axis_size("z"), lax.axis_index("z")
    count = ends.shape[0] // 2
    carry = jnp.zeros_like(ends[:count])
    for far in range(chips - 1, 0, -1):
        step = -far if reverse else far
        there = lax.ppermute(ends, "z", [(i, (i + step) % chips) for i in range(chips)])
        reached = here + far < chips if reverse else here >= far
        carry = jnp.where(reached, there[count:] + there[:count] * carry, carry)
    return carry


def flip(part, axis, bit):
    count = lax.axis_size(axis)
    return lax.ppermute(part, axis, [(i, i ^ bit) for i in range(count)])


def bits_of(axis):
    return [1 << k for k in range(lax.axis_size(axis).bit_length() - 1)]


def half_rows(rows):
    return -(-rows // 32) * 16


def gather_groups(part, *earlier):
    if lax.axis_size("dp") == 4:
        half = half_rows(part.shape[0])
        one, two = flip(part, "dp", 1), flip(part, "dp", 2)
        if earlier:
            one, two = after(one, *earlier), after(two, *earlier)
        three = jnp.concatenate(
            [flip(one[:half], "dp", 2), flip(two[half:], "dp", 1)], axis=0
        )
        return [part, one, two, three]
    blocks = [part]
    for bit in bits_of("dp"):
        blocks = blocks + [flip(block, "dp", bit) for block in blocks]
    return blocks


def scatter_groups(blocks, *earlier):
    if len(blocks) == 4:
        half = half_rows(blocks[0].shape[0])
        upper = flip(blocks[3][:half], "dp", 1)
        lower = flip(blocks[3][half:], "dp", 2)
        two = jnp.concatenate([add_low(blocks[2][:half], upper), blocks[2][half:]], axis=0)
        one = jnp.concatenate([blocks[1][:half], add_low(blocks[1][half:], lower)], axis=0)
        if earlier:
            one, two = after(one, *earlier), after(two, *earlier)
        return [blocks[0], flip(one, "dp", 1), flip(two, "dp", 2)]
    for bit in reversed(bits_of("dp")):
        blocks = [
            add_low(block, flip(other, "dp", bit))
            for block, other in zip(blocks[:bit], blocks[bit:])
        ]
    return blocks


def add_parts(parts):
    total = parts[0].astype(f32)
    for part in parts[1:]:
        total = total + part.astype(f32)
    return total


def add_low(left, right):
    return (left.astype(f32) + right.astype(f32)).astype(bf16)


def sum_over(part, axes):
    for axis in axes:
        for bit in bits_of(axis):
            part = part + flip(part, axis, bit)
    return part


def place_groups(blocks):
    group, rows = lax.axis_index("dp"), blocks[0].shape[0]
    whole = jnp.zeros((len(blocks) * rows,) + blocks[0].shape[1:], blocks[0].dtype)
    for b, block in enumerate(blocks):
        whole = lax.dynamic_update_slice_in_dim(whole, block, (group ^ b) * rows, 0)
    return whole


def take_groups(whole, axis):
    count, group = lax.axis_size("dp"), lax.axis_index("dp")
    size = whole.shape[axis] // count
    return [
        lax.dynamic_slice_in_dim(whole, (group ^ b) * size, size, axis) for b in range(count)
    ]


def sequence_pieces():
    groups, peers = lax.axis_size("dp"), lax.axis_size("z") * 2
    return [[g * peers + j for g in range(groups)] for j in range(peers)]


def plane_pieces():
    groups, chips = lax.axis_size("dp"), lax.axis_size("z")
    return [
        [(g * chips + z) * 2 + core for z in range(chips)]
        for g in range(groups)
        for core in range(2)
    ]


def split_kernel(kinds, piece, table, weight_ref, split_ref, *rest_refs):
    rows, every, depth = weight_ref.shape
    whole = [weight_ref[:, k, :] for k in range(every)]
    for j, pieces in enumerate(table):
        own = [
            whole[k][:, p * piece : (p + 1) * piece] for k in range(kinds) for p in pieces
        ]
        split_ref[j * rows : (j + 1) * rows, :] = jnp.concatenate(own, axis=1).astype(bf16)
    for k, rest_ref in zip(range(kinds, every), rest_refs):
        part = depth // len(table)
        for j in range(len(table)):
            rest_ref[j * rows : (j + 1) * rows, :] = whole[k][
                :, j * part : (j + 1) * part
            ].astype(bf16)


def split_columns(weight, kinds, piece, table):
    rows, every, depth = weight.shape
    shapes = [jax.ShapeDtypeStruct((len(table) * rows, kinds * len(table[0]) * piece), bf16)]
    shapes += [
        jax.ShapeDtypeStruct((len(table) * rows, depth // len(table)), bf16)
    ] * (every - kinds)
    return pl.pallas_call(
        functools.partial(split_kernel, kinds, piece, table),
        out_shape=shapes,
        compiler_params=pltpu.CompilerParams(vmem_limit_bytes=VMEM_BYTES),
        name="split_columns",
    )(weight)


def join_kernel(kinds, piece, table, own_ref, *refs):
    rest_refs, out_ref = refs[:-1], refs[-1]
    rows, every, depth = out_ref.shape
    place = {p: (j, q) for j, pieces in enumerate(table) for q, p in enumerate(pieces)}
    count = len(table[0])
    own = [own_ref[j * rows : (j + 1) * rows, :].astype(f32) for j in range(len(table))]
    for k in range(kinds):
        pieces = []
        for p in range(len(place)):
            j, q = place[p]
            pieces.append(own[j][:, (k * count + q) * piece : (k * count + q + 1) * piece])
        out_ref[:, k, :] = jnp.concatenate(pieces, axis=1)
    for k, rest_ref in zip(range(kinds, every), rest_refs):
        out_ref[:, k, :] = rest_ref[...]


def join_columns(own, kinds, piece, table, *rest):
    shape = (own.shape[0] // len(table), kinds + len(rest), len(table) * len(table[0]) * piece)
    return pl.pallas_call(
        functools.partial(join_kernel, kinds, piece, table),
        out_shape=jax.ShapeDtypeStruct(shape, f32),
        compiler_params=pltpu.CompilerParams(vmem_limit_bytes=VMEM_BYTES),
        name="join_columns",
    )(own, *rest)


def after_kernel(*refs):
    pass


def after(value, *earlier):
    return pl.pallas_call(
        after_kernel,
        out_shape=jax.ShapeDtypeStruct(value.shape, value.dtype),
        in_specs=[pl.BlockSpec(memory_space=pl.ANY)] * (1 + len(earlier)),
        out_specs=pl.BlockSpec(memory_space=pl.ANY),
        input_output_aliases={0: 0},
        name="after",
    )(value, *earlier)


def dot(left, right, dims):
    return lax.dot_general(left, right, (dims, ((), ())), preferred_element_type=f32)


def body(
    tokens,
    out_cotangent,
    counts,
    forget_gap,
    mixer_weight,
    expand_weight,
    shrink_weight,
    norm_gains,
    mixer_first,
    mixer_second,
    expand_first,
    expand_second,
    shrink_first,
    shrink_second,
    gains_first,
    gains_second,
):
    nd, chips = lax.axis_size("dp"), lax.axis_size("z")
    group, core = lax.axis_index("dp"), lax.axis_index("core")
    slots, depth = tokens.shape
    rows = mixer_weight.shape[0]
    hid_rows = shrink_weight.shape[0]
    width = chips * rows
    hid = nd * hid_rows
    plane_rows = 2 * nd * slots
    core_low = core.astype(jnp.int32).reshape(1)

    def own_columns(vector):
        pieces = vector.reshape(nd, chips, 2, rows)
        return lax.dynamic_slice(pieces, (group, 0, core, 0), (1, chips, 1, rows)).reshape(1, width)

    def turn(whole, first, second):
        pieces = whole.reshape(slots, first, second, 2 * rows)
        return pieces.transpose(0, 2, 1, 3).reshape(slots, depth)

    lead_blocks, trail_low = split_columns(mixer_weight, 3, rows, plane_pieces())
    (expand_blocks,) = split_columns(expand_weight, 2, hid_rows, sequence_pieces())

    valid_here = (lax.iota(jnp.int32, slots) < counts[0, 0]).astype(f32)[:, None]
    inputs = tokens.astype(f32)
    scale_one = rms_scale(inputs)
    normed_one = inputs * scale_one
    input_low = turn((normed_one * norm_gains[0]).astype(bf16), nd, chips)
    cotangent_low = (out_cotangent.astype(f32) * valid_here).astype(bf16)

    lead_own = swap(lead_blocks, PLANE)
    expand_own = swap(after(expand_blocks, lead_own), SEQUENCE)
    input_low = jnp.concatenate([input_low, pad_columns(valid_here.astype(bf16))], axis=1)
    input_all, _ = gather_plane(after(input_low, lead_own))
    valid = input_all[:, depth : depth + 1].astype(f32)
    input_all = input_all[:, :depth]
    shrink = place_groups(gather_groups(after(shrink_weight.astype(bf16), valid)))
    expand = place_groups(gather_groups(after(expand_own, shrink)))
    mixer_own = jnp.concatenate([lead_own, trail_low], axis=1)
    mixer_near = gather_chips(after(mixer_own, expand_own))
    cotangent_all = gather_tokens(after(cotangent_low, mixer_near))
    mixer_near = after(mixer_near, valid, expand)
    lead = mixer_near[:, : 3 * width]
    trail = mixer_near[:, 3 * width :].reshape(chips, 2 * nd, rows, width)
    trail = trail.transpose(0, 2, 1, 3).reshape(width, depth)

    gap = own_columns(forget_gap)
    gain = own_columns(norm_gains[1])
    logits = dot(input_all, lead, ((1,), (0,)))
    square, low_square = ((plane_rows, width), f32), ((plane_rows, width), bf16)
    ends_shape = ((2 * nd, width), f32)
    decay, local, ends = call_kernel(
        recur_forward_kernel,
        "recur_forward",
        [square, square, ends_shape],
        core_low,
        logits,
        valid,
        gap,
    )
    carry = chain_chips(ends, False)
    hidden, before, mix, squares = call_kernel(
        recur_mix_kernel,
        "recur_mix",
        [square, square, low_square, ((plane_rows, 1), f32)],
        core_low,
        logits,
        decay,
        local,
        carry,
        gain,
    )
    mixed_part = dot(mix, trail, ((1,), (0,))).astype(bf16)
    mixed_part = jnp.concatenate([mixed_part, pad_columns(split_low(squares))], axis=1)
    mixed_sum = add_parts(scatter_plane(mixed_part, cotangent_all))
    scale_two = lax.rsqrt(
        (mixed_sum[:, depth : depth + 1] + mixed_sum[:, depth + 1 : depth + 2]) / depth + norm_eps
    )
    mixed = mixed_sum[:, :depth] * scale_two
    residual = inputs + mixed
    scale_three = rms_scale(residual)
    normed_three = residual * scale_three
    feed_low = (normed_three * norm_gains[2]).astype(bf16)
    feed_all = gather_tokens(after(feed_low, cotangent_all))
    expanded = dot(feed_all, expand, ((1,), (0,)))
    gate, up = expanded[:, :hid], expanded[:, hid:]
    gate_silu = jax.nn.silu(gate)
    product_low = (gate_silu * up).astype(bf16)
    grad_product = dot(cotangent_all, shrink, ((1,), (1,)))
    grad_expanded = jnp.concatenate(
        [grad_product * up * silu_slope(gate), grad_product * gate_silu], axis=1
    ).astype(bf16)
    feed_part = dot(grad_expanded, expand, ((1,), (1,))).astype(bf16)
    grad_feed = scatter_tokens(feed_part)
    gain_three = jnp.sum(grad_feed * normed_three, 0)
    grad_residual = cotangent_low.astype(f32) + rms_back(
        grad_feed * norm_gains[2], normed_three, scale_three
    )
    residual_low = grad_residual.astype(bf16)
    mean_two = jnp.mean(residual_low.astype(f32) * mixed, axis=-1, keepdims=True)
    extras = pad_columns(jnp.concatenate([split_low(scale_two), split_low(mean_two)], axis=1))

    def owner_parts(left, right):
        return [
            dot(block, right, ((0,), (0,))).astype(bf16) for block in take_groups(left, 1)
        ]

    expand_sum = add_parts(scatter_groups(owner_parts(feed_all, grad_expanded))).astype(bf16)
    expand_columns = swap(expand_sum, SEQUENCE)
    back_all, back_near = gather_plane(
        after(jnp.concatenate([residual_low, extras], axis=1), expand_sum), expand_columns
    )
    out_part = dot(product_low, shrink, ((1,), (0,))).astype(bf16)
    out_sum = scatter_tokens(after(out_part, back_near))
    block_output = ((residual + out_sum) * valid_here).astype(bf16)
    residual_back = back_all[:, :depth]
    extras = back_all[:, depth : depth + 4].astype(f32)
    scale_all = extras[:, 0:1] + extras[:, 1:2]
    mean_all = extras[:, 2:3] + extras[:, 3:4]

    grad_mix = dot(residual_back, trail, ((1,), (1,)))
    decay, local, out_grad, mix_low, ends, gain_two = call_kernel(
        recur_reverse_kernel,
        "recur_reverse",
        [square, square, low_square, low_square, ends_shape, ((1, width), f32)],
        core_low,
        logits,
        hidden,
        grad_mix,
        valid,
        scale_all,
        mean_all,
        gap,
        gain,
    )
    carry = chain_chips(ends, True)
    (grad_projected,) = call_kernel(
        recur_finish_kernel,
        "recur_finish",
        [((plane_rows, 3 * width), bf16)],
        None,
        logits,
        before,
        valid,
        decay,
        local,
        carry,
        out_grad,
        gap,
    )
    trail_part = dot(mix_low, residual_back, ((0,), (0,))).astype(bf16)
    lead_part = dot(input_all, grad_projected, ((0,), (0,))).astype(bf16)
    lead_part = after(lead_part, out_sum)
    lead_sum = scatter_chips(lead_part)
    trail_grad = scatter_chips(after(trail_part, lead_sum))
    input_part = dot(after(grad_projected, lead_part), lead, ((1,), (1,))).astype(bf16)
    input_parts = scatter_plane(input_part)
    token_grad, gain_one = call_kernel(
        functools.partial(finish_input_kernel, nd, chips),
        "finish_input",
        [((slots, depth), bf16), ((1, depth), f32)],
        None,
        tokens,
        norm_gains,
        grad_residual,
        *input_parts,
    )
    gain_one = gain_one[0]
    shrink_part = dot(product_low, after(cotangent_all, input_part), ((0,), (0,))).astype(bf16)
    shrink_grad = add_parts(scatter_groups(take_groups(shrink_part, 0)))

    expand_grad = join_columns(
        after(expand_columns, input_part), 2, hid_rows, sequence_pieces()
    )
    lead_columns = swap(lead_sum, PLANE)

    gain_two_full = lax.dynamic_update_slice(
        jnp.zeros((nd, chips, 2, rows), f32),
        gain_two.reshape(1, chips, 1, rows),
        (group, 0, core, 0),
    ).reshape(depth)
    mixer_grad = join_columns(lead_columns, 3, rows, plane_pieces(), trail_grad.astype(f32))
    expand_first_new, expand_second_new, expand_update = adam_direction(
        expand_weight, expand_grad, expand_first, expand_second
    )
    shrink_first_new, shrink_second_new, shrink_update = adam_direction(
        shrink_weight, shrink_grad, shrink_first, shrink_second
    )
    mixer_first_new, mixer_second_new, mixer_update = adam_direction(
        mixer_weight, mixer_grad, mixer_first, mixer_second
    )
    squares_here = jnp.concatenate(
        [
            squares_of(mixer_weight),
            squares_of(expand_weight),
            squares_of(shrink_weight[:, None]),
            squares_of(mixer_update),
            squares_of(expand_update),
            squares_of(shrink_update[:, None]),
        ]
    )
    summed = sum_over(
        after(
            jnp.stack([gain_one, gain_two_full, gain_three, jnp.pad(squares_here, (0, depth - 14))]),
            block_output,
        ),
        ("dp", "z", "core"),
    )
    gains_grad = summed[:3]
    weight_sq, update_sq = summed[3, :7], summed[3, 7:14]
    gains_first_new, gains_second_new, gains_update = adam_direction(
        norm_gains, gains_grad, gains_first, gains_second
    )
    mixer_weight_new = apply_trust(
        mixer_weight, mixer_update, weight_sq[0:4], update_sq[0:4], (1, 4, 1)
    )
    expand_weight_new = apply_trust(
        expand_weight, expand_update, weight_sq[4:6], update_sq[4:6], (1, 2, 1)
    )
    shrink_weight_new = apply_trust(
        shrink_weight, shrink_update, weight_sq[6], update_sq[6], (1, 1)
    )
    gain_weight_sq = jnp.sum(norm_gains * norm_gains, axis=1)
    gain_update_sq = jnp.sum(gains_update * gains_update, axis=1)
    gains_new = apply_trust(norm_gains, gains_update, gain_weight_sq, gain_update_sq, (3, 1))
    weight_norms = jnp.sqrt(jnp.concatenate([weight_sq, gain_weight_sq]))
    update_norms = jnp.sqrt(jnp.concatenate([update_sq, gain_update_sq]))
    trust_norms = jnp.stack([weight_norms, update_norms])
    return (
        block_output,
        token_grad,
        mixer_grad,
        mixer_first_new,
        mixer_second_new,
        mixer_weight_new,
        expand_grad,
        expand_first_new,
        expand_second_new,
        expand_weight_new,
        shrink_grad,
        shrink_first_new,
        shrink_second_new,
        shrink_weight_new,
        gains_grad,
        gains_first_new,
        gains_second_new,
        gains_new,
        trust_norms,
    )


def solution(mesh):
    groups, peers = mesh.devices.shape
    devices = mesh.devices.reshape(groups, peers // 2, 2)
    return jax.shard_map(
        body,
        mesh=jax.sharding.Mesh(devices, ("dp", "z", "core")),
        in_specs=(
            P(("dp", "z", "core"), None),
            P(("dp", "z", "core"), None),
            P("dp", ("z", "core")),
            P(),
            P(("dp", "z", "core"), None, None),
            P(("dp", "z", "core"), None, None),
            P(("dp", "z", "core"), None),
            P(),
            P(("dp", "z", "core"), None, None),
            P(("dp", "z", "core"), None, None),
            P(("dp", "z", "core"), None, None),
            P(("dp", "z", "core"), None, None),
            P(("dp", "z", "core"), None),
            P(("dp", "z", "core"), None),
            P(),
            P(),
        ),
        out_specs=(
            P(("dp", "z", "core"), None),
            P(("dp", "z", "core"), None),
            P(("dp", "z", "core"), None, None),
            P(("dp", "z", "core"), None, None),
            P(("dp", "z", "core"), None, None),
            P(("dp", "z", "core"), None, None),
            P(("dp", "z", "core"), None, None),
            P(("dp", "z", "core"), None, None),
            P(("dp", "z", "core"), None, None),
            P(("dp", "z", "core"), None, None),
            P(("dp", "z", "core"), None),
            P(("dp", "z", "core"), None),
            P(("dp", "z", "core"), None),
            P(("dp", "z", "core"), None),
            P(),
            P(),
            P(),
            P(),
            P(),
        ),
        check_vma=False,
    )
```
